128 devices in a mesh: sample: 4 (over z), cent: 32 (over x, y, core).
Axes of the slice: x: 4, y: 4, z: 4, core: 2. Of those that a mesh axis runs over, the one named last changes fastest.
Arguments:
- embeddings: bfloat16 [2097152, 256], P(('sample', 'cent')), may hold values from -6 to 6
- route: int32 [2097152, 1], P(('sample', 'cent')), may hold values from 0 to 127; in each aligned block of 16384 rows (0 to 16383, 16384 to 32767, ...) at most 256 rows name the same one
- offset: int32 [2097152], P(('sample', 'cent')), may hold values from 0 to 511
- centroids: float32 [65536, 256], P('cent'), may hold values from -6 to 6
Outputs:
- updated: float32 [65536, 256], P('cent')
The draws below stay inside these ranges and needn't reach their ends.
Inputs may be any that keep to these rules, and one draw needn't show every extreme that they name: Of the 16384 rows of one device (aligned blocks), at most 256 name one route; route r holds centroids r * 512 to (r + 1) * 512 - 1.
All inputs are finite; a program needn't handle non-finite values.
Results may differ from the reference program's by a relative error of at most 0.0003.
Values may be sent and summed in bfloat16 or wider, within the bound.
A program may use at most 128 MiB of HBM per device.

```python
import math
import jax
import jax.numpy as jnp
import numpy as np

DW = 256
K = 65536
ROW_DEV = 16384
ROWS = 2097152
SUB = 512
CAP = 256
DEVICES = 128


def place_ends(entries, key, least, top_value):
    shape = entries.shape
    spot = [jax.random.randint(jax.random.fold_in(key, axis), (), 0, shape[axis]) for axis in range(len(shape))]
    entries = entries.at[tuple(spot)].set(least)
    longest = shape.index(max(shape))
    spot[longest] = (spot[longest] + 1) % shape[longest]
    return entries.at[tuple(spot)].set(top_value)


def steps_of(stream_key, shape, split, least, top_value):
    def one(dim, blocks):
        steps = jax.random.uniform(jax.random.fold_in(jax.random.fold_in(stream_key, 6), dim), (blocks,), jnp.float32, least / len(split), top_value / len(split))
        return jnp.repeat(jnp.exp(steps), shape[dim] // blocks).reshape((-1,) + (1,) * (len(shape) - dim - 1))

    loudness = one(*split[0])
    for cut in split[1:]:
        loudness = loudness * one(*cut)
    return loudness


def rank_table(amount, slope):
    loads = [(1 << 20) // math.isqrt(grade ** slope) + 1 for grade in range(1, amount + 1)]
    deviation = 1 + sum(loads) // (1 << 30)
    return np.cumsum(np.array([max(1, weight // deviation) for weight in loads]))


def ranked_ids(key, shape, number_of, lean):
    listing = rank_table(number_of, lean)
    ticket = jax.random.randint(jax.random.fold_in(key, 1), shape, 0, int(listing[number_of - 1]))
    rank = jnp.searchsorted(jnp.asarray(listing, jnp.int32), ticket, side="right")
    return jax.random.permutation(jax.random.fold_in(key, 2), number_of)[rank].astype(jnp.int32)


def deal_out(rng, own, number, rows, amount, top, limit, skew):
    order = jax.random.permutation(rng, amount)
    crowded, common = shares(amount, rows * top, limit, skew, True), shares(amount, rows * top, limit, skew, False)
    places = jnp.arange(amount)

    def named(sizes, rotation):
        used = int((sizes > 0).sum())
        fixed = max(1, used // 4)
        moved = fixed + (places - fixed + rotation * (used - fixed)) % max(1, amount - fixed)
        return jnp.zeros((amount,), jnp.int32).at[order[jnp.where(places < fixed, places, moved)]].set(jnp.asarray(sizes, jnp.int32))

    sizes = jnp.where(number % 4 == 0, named(crowded, number // 4), named(common, number - number // 4 - 1))
    mixed = jax.random.permutation(jax.random.fold_in(own, 3), amount)
    giver, sink = mixed[0:amount // 2 * 2:2], mixed[1:amount // 2 * 2:2]
    slack = jnp.minimum(sizes[giver] - 1, limit - sizes[sink]) // 2
    slack = jnp.where((giver == order[0]) | (sink == order[0]) | (sizes[sink] == 0), 0, jnp.maximum(slack, 0))
    moved = jax.random.randint(jax.random.fold_in(own, 4), (amount // 2,), 0, 1 << 20) % (slack + 1)
    sizes = sizes.at[giver].add(-moved).at[sink].add(moved)
    labels = jnp.searchsorted(jnp.cumsum(sizes), jnp.arange(rows * top), side="right").astype(jnp.int32)
    table = labels.reshape(top, rows).T
    table = table[jax.random.permutation(jax.random.fold_in(own, 1), rows)]
    rotation = jax.random.randint(jax.random.fold_in(own, 2), (rows, 1), 0, top)
    return jnp.take_along_axis(table, (jnp.arange(top)[None, :] + rotation) % top, axis=1)


def shares(count, total, reach, lean, full):
    portions = [(1 << 20) // math.isqrt(standing ** lean) + 1 for standing in range(1, count + 1)]
    largest = reach if full else min(reach, max(-(-total // count), total * portions[0] // sum(portions)))
    least = 1 if total - largest >= count - 1 else 0
    given, spare = [largest] + [least] * (count - 1), total - largest - least * (count - 1)
    while spare > 0:
        movable = [i for i in range(1, count) if given[i] < largest] or [i for i in range(1, count) if given[i] < reach]
        whole, remaining = sum([portions[i] for i in movable]), spare
        for i in movable:
            more = min(reach - given[i], max(1, remaining * portions[i] // whole), spare)
            given[i] = given[i] + more
            spare = spare - more
    return np.array(given)


def centred(stream_key, shape, spread, most, pieces=(), dtype=jnp.bfloat16):
    array = spread * jax.random.normal(stream_key, shape, jnp.float32)
    if pieces:
        array = array * steps_of(stream_key, shape, pieces, -0.22, 0.18)
    return jnp.clip(array, -most, most).astype(dtype)


def setup_inputs(seed: int = 0) -> dict:
    splits = jax.random.split(jax.random.key(seed), 5)
    embeddings = centred(splits[0], (ROWS, DW), 1.0, 6.0, ((0, 128),))
    route_keys = jax.random.split(jax.random.fold_in(splits[1], 1), ROWS // ROW_DEV)
    route_turns = jax.random.permutation(jax.random.fold_in(splits[1], 3), ROWS // ROW_DEV)
    route = jax.vmap(lambda own, number: deal_out(jax.random.fold_in(splits[1], 2), own, number, ROW_DEV, DEVICES, 1, CAP, 2))(route_keys, route_turns).reshape((ROWS, 1))
    offset = place_ends(ranked_ids(splits[2], (ROWS,), SUB, 3), jax.random.fold_in(splits[2], 3), 0, SUB - 1).astype(jnp.int32)
    centroids = centred(splits[3], (K, DW), 1.0, 6.0, ((0, 32),), jnp.float32)
    return {"embeddings": embeddings, "route": route, "offset": offset, "centroids": centroids}


def reference(embeddings, route, offset, centroids):
    assign = (route[:, 0] * SUB + offset).astype(jnp.int32)
    sums = jax.ops.segment_sum(embeddings.astype(jnp.float32), assign, num_segments=K)
    counts = jax.ops.segment_sum(jnp.ones(assign.shape, jnp.float32), assign, num_segments=K)
    safe = jnp.maximum(counts, 1.0)
    return jnp.where(counts[:, None] > 0.0, sums / safe[:, None], centroids)
```

```python
import functools

import jax
import jax.numpy as jnp
from jax import lax
from jax.experimental import pallas as pl
from jax.experimental.pallas import tpu as pltpu
from jax.sharding import PartitionSpec as P

MESH = pl.DeviceIdType.MESH
K = 65536
WIDTH = 256
ROUTES = 128
SUB = 512
CAP = 256
ROWS = 16384
CHUNK = 512
CHUNKS = ROWS // CHUNK
SLOTS = ROUTES * CAP
PART = 1024
F32, BF16, I32 = jnp.float32, jnp.bfloat16, jnp.int32


def place_of(route):
    quarter = route & 3
    core = (route >> 2) & 1
    y = (route >> 3) & 3
    x = route >> 5
    by_y = (quarter == 1) | ((quarter == 3) & (core == 1))
    ring = jnp.where(by_y, y, x)
    other = jnp.where(by_y, x, y)
    return quarter * 32 + ring * 8 + core * 4 + other


def index_kernel(route, offset, x, slots, labels, counts, pairs, upper, weave, base, found):
    step = pl.program_id(0)

    @pl.when(step == 0)
    def _():
        row = lax.broadcasted_iota(I32, (CHUNK, CHUNK), 0)
        col = lax.broadcasted_iota(I32, (CHUNK, CHUNK), 1)
        upper[...] = (row < col).astype(F32).astype(BF16)
        row = lax.broadcasted_iota(I32, (256, 256), 0)
        col = lax.broadcasted_iota(I32, (256, 256), 1)
        weave[...] = (col == (row >> 1) + (row & 1) * 128).astype(F32).astype(BF16)
        base[...] = jnp.zeros_like(base)
        found[...] = jnp.zeros_like(found)
        counts[...] = jnp.zeros_like(counts)

    named = route[pl.ds(step, 1), :]
    within = offset[pl.ds(step, 1), :]
    place = place_of(named)
    lane_dot = (((1,), (1,)), ((), ()))

    routes = lax.broadcasted_iota(I32, (ROUTES, CHUNK), 0)
    mark = routes == place
    mark_f = mark.astype(F32)
    mark_b = mark_f.astype(BF16)
    before = jnp.dot(mark_b, upper[...], preferred_element_type=F32) + base[:, :1]
    rank = jnp.sum(jnp.where(mark, before, 0.0), axis=0, keepdims=True).astype(I32)
    slots[pl.ds(step, 1), :] = place * CAP + rank
    base[...] = base[...] + jnp.sum(mark_f, axis=1, keepdims=True)

    ranks = lax.broadcasted_iota(I32, (CAP, CHUNK), 0)
    value = jnp.where(ranks == rank, (within - 256).astype(F32), 0.0).astype(BF16)
    found[...] += lax.dot_general(mark_b, value, lane_dot, preferred_element_type=F32)

    natural = (routes == named).astype(F32).astype(BF16)
    offsets = lax.broadcasted_iota(I32, (SUB, CHUNK), 0)
    hit = (offsets == within).astype(F32).astype(BF16)
    counts[...] += lax.dot_general(natural, hit, lane_dot, preferred_element_type=F32)

    for part in range(CHUNK // 128):
        block = x[part * 128:(part + 1) * 128, :]
        stacked = jnp.concatenate([block[:, :128], block[:, 128:]], axis=0)
        woven = jnp.dot(weave[...], stacked, preferred_element_type=F32)
        pairs[part * 256:(part + 1) * 256, :] = woven.astype(BF16)

    @pl.when(step == CHUNKS - 1)
    def _():
        lanes = lax.broadcasted_iota(I32, (ROUTES, CAP), 1)
        labels[...] = jnp.where(lanes < base[:, :1].astype(I32), found[...].astype(I32) + 256, -1)


def index_call(route, offset, x):
    whole = lambda shape: pl.BlockSpec(shape, lambda i: (0,) * len(shape))
    return pl.pallas_call(
        index_kernel,
        grid=(CHUNKS,),
        out_shape=[
            jax.ShapeDtypeStruct((CHUNKS, CHUNK), I32),
            jax.ShapeDtypeStruct((ROUTES, CAP), I32),
            jax.ShapeDtypeStruct((ROUTES, SUB), F32),
            jax.ShapeDtypeStruct((2 * ROWS, 128), BF16),
        ],
        in_specs=[
            whole((CHUNKS, CHUNK)),
            whole((CHUNKS, CHUNK)),
            pl.BlockSpec((CHUNK, WIDTH), lambda i: (i, 0)),
        ],
        out_specs=[
            whole((CHUNKS, CHUNK)),
            whole((ROUTES, CAP)),
            whole((ROUTES, SUB)),
            pl.BlockSpec((2 * CHUNK, 128), lambda i: (i, 0)),
        ],
        scratch_shapes=[
            pltpu.VMEM((CHUNK, CHUNK), BF16),
            pltpu.VMEM((256, 256), BF16),
            pltpu.VMEM((ROUTES, 128), F32),
            pltpu.VMEM((ROUTES, CAP), F32),
        ],
        compiler_params=pltpu.CompilerParams(vmem_limit_bytes=32 << 20),
    )(route, offset, x)


def place_kernel(slots, x, out, rows, packed, blank, in_sem, zero_sem, out_sem):
    loads = []
    for part in range(ROWS // PART):
        span = pl.ds(part * PART, PART)
        loads.append(pltpu.make_async_copy(x.at[span], rows.at[span], in_sem.at[part]))
        loads[-1].start()
    blank[...] = jnp.zeros_like(blank)
    clears = []
    for part in range(SLOTS // PART):
        clears.append(pltpu.make_async_copy(blank, packed.at[pl.ds(part * PART, PART)], zero_sem.at[part]))
        clears[-1].start()
    for clear in clears:
        clear.wait()
    for part, load in enumerate(loads):
        load.wait()

        def sixteen(i, _):
            for u in range(16):
                j = part * PART + i * 16 + u
                packed[slots[j]] = rows[j]
            return 0

        lax.fori_loop(0, PART // 16, sixteen, 0)
    stores = []
    for part in range(SLOTS // PART):
        span = pl.ds(part * PART, PART)
        stores.append(pltpu.make_async_copy(packed.at[span], out.at[span], out_sem.at[part]))
        stores[-1].start()
    for store in stores:
        store.wait()


def place_call(slots, x):
    return pl.pallas_call(
        place_kernel,
        out_shape=jax.ShapeDtypeStruct((SLOTS, 2, 128), BF16),
        in_specs=[pl.BlockSpec(memory_space=pltpu.SMEM), pl.BlockSpec(memory_space=pl.ANY)],
        out_specs=pl.BlockSpec(memory_space=pl.ANY),
        scratch_shapes=[
            pltpu.VMEM((ROWS, 2, 128), BF16),
            pltpu.VMEM((SLOTS, 2, 128), BF16),
            pltpu.VMEM((PART, 2, 128), BF16),
            pltpu.SemaphoreType.DMA((ROWS // PART,)),
            pltpu.SemaphoreType.DMA((SLOTS // PART,)),
            pltpu.SemaphoreType.DMA((SLOTS // PART,)),
        ],
        compiler_params=pltpu.CompilerParams(vmem_limit_bytes=56 << 20),
    )(slots, x)


def device_at(x, y, z, core):
    return {"sample": z, "cent": (x * 4 + y) * 2 + core}


def reduce_kernel(rows, labels, out, got, got_labels, partial, got2, second, got3, third, crossed,
                  s1, r1, sl, rl, s2, r2, s3, r3, s4, r4, s5, r5, own):
    z = lax.axis_index("sample")
    cent = lax.axis_index("cent")
    x, y, core = cent // 8, (cent // 2) % 4, cent % 2
    at = {"x": x, "y": y, "z": z}

    def along(axis, distance, core_to=None):
        to = dict(at)
        to[axis] = (to[axis] + distance) % 4
        return device_at(to["x"], to["y"], to["z"], core if core_to is None else core_to)

    def by_core(distance):
        return device_at((x + distance * core) % 4, (y + distance * (1 - core)) % 4, z, core)

    barrier = pltpu.get_barrier_semaphore()
    other = (core + 1) % 2
    pl.semaphore_signal(barrier, inc=1, device_id=device_at(x, y, z, other), device_id_type=MESH)
    for axis in "xyz":
        for distance in (1, 2, 3):
            for core_to in (core, other):
                pl.semaphore_signal(barrier, inc=1, device_id=along(axis, distance, core_to), device_id_type=MESH)
    pl.semaphore_wait(barrier, 19)

    hops = [(2, 0), (2, 1), (1, 0), (3, 0), (1, 1), (3, 1), (0, 1)]
    first = {}
    for j, (distance, flip) in enumerate(hops):
        for q in (2, 0, 1, 3):
            core_to = (core + flip) % 2
            if q == 3:
                ring = x * (1 - core_to) + y * core_to
                device = device_at((x + distance * (1 - core_to)) % 4, (y + distance * core_to) % 4, z, core_to)
            else:
                axis = "xyz"[q]
                ring = at[axis]
                device = along(axis, distance, core_to)
            to = ((ring + distance) % 4) * 2 + core_to
            mine = ring * 2 + core
            pair = []
            for src, dst, ss, rs in ((rows, got, s1, r1), (labels, got_labels, sl, rl)):
                pair.append(pltpu.make_async_remote_copy(
                    src_ref=src.at[q, to], dst_ref=dst.at[q, mine], send_sem=ss.at[q, j], recv_sem=rs.at[q, j],
                    device_id=device, device_id_type=MESH))
                pair[-1].start()
            first[q, j] = pair
    local = {}
    for q in range(4):
        ring = x * (1 - core) + y * core if q == 3 else at["xyz"[q]]
        mine = ring * 2 + core
        local[q] = [pltpu.make_async_copy(rows.at[q, mine], got.at[q, mine], own.at[q, 0]),
                    pltpu.make_async_copy(labels.at[q, mine], got_labels.at[q, mine], own.at[q, 1])]
        for copy in local[q]:
            copy.start()

    split_row = lax.broadcasted_iota(I32, (256, 256), 0)
    split_col = lax.broadcasted_iota(I32, (256, 256), 1)
    split = (split_col == (split_row % 128) * 2 + split_row // 128).astype(F32).astype(BF16)

    def add_up(q):
        def one(other_at, _):
            def add(src, total):
                name = got_labels[q, src, pl.ds(other_at, 1), :]
                parts = []
                for half in range(2):
                    block = got[q, src, other_at, half * 256:(half + 1) * 256, :]
                    flat = jnp.dot(split, block, preferred_element_type=F32).astype(BF16)
                    parts.append(jnp.concatenate([flat[:128], flat[128:]], axis=1))
                flat = jnp.concatenate(parts, axis=0)
                hit = (lax.broadcasted_iota(I32, (SUB, CAP), 0) == name).astype(F32).astype(BF16)
                return total + jnp.dot(hit, flat, preferred_element_type=F32)

            total = lax.fori_loop(0, 8, add, jnp.zeros((SUB, WIDTH), F32))
            if q == 0:
                for part in range(4):
                    partial[q, part, pl.ds(pl.multiple_of(other_at * 128, 128), 128), :] = total[part * 128:(part + 1) * 128]
            else:
                partial[q, other_at] = total
            return 0

        lax.fori_loop(0, 4, one, 0)

    second_axis = {0: "z", 1: "x", 2: "y"}
    second_copies = {}

    def start_second(q):
        here = y * (1 - core) + x * core if q == 3 else at[second_axis[q]]
        for distance in (2, 1, 3):
            device = by_core(distance) if q == 3 else along(second_axis[q], distance)
            copy = pltpu.make_async_remote_copy(
                src_ref=partial.at[q, (here + distance) % 4], dst_ref=got2.at[q, distance - 1],
                send_sem=s2.at[q, distance - 1], recv_sem=r2.at[q, distance - 1], device_id=device, device_id_type=MESH)
            copy.start()
            second_copies[q, distance] = copy

    third_axis = {0: "y", 1: "z", 2: "x", 3: "z"}
    third_copies = {}

    def start_third(q):
        here = y * (1 - core) + x * core if q == 3 else at[second_axis[q]]
        for distance in (2, 1, 3):
            second_copies[q, distance].wait()
        second[q] = partial[q, here] + got2[q, 0] + got2[q, 1] + got2[q, 2]
        here = at[third_axis[q]]
        for distance in (2, 1, 3):
            span = pl.ds(pl.multiple_of(((here + distance) % 4) * 128, 128), 128)
            copy = pltpu.make_async_remote_copy(
                src_ref=second.at[q, span], dst_ref=got3.at[q, distance - 1],
                send_sem=s3.at[q, distance - 1], recv_sem=r3.at[q, distance - 1],
                device_id=along(third_axis[q], distance), device_id_type=MESH)
            copy.start()
            third_copies[q, distance] = copy

    last_copies = {}

    def start_last(q):
        here = at[third_axis[q]]
        for distance in (2, 1, 3):
            third_copies[q, distance].wait()
        span = pl.ds(pl.multiple_of(here * 128, 128), 128)
        third[q] = second[q, span, :] + got3[q, 0] + got3[q, 1] + got3[q, 2]
        target = crossed.at[z] if q == 2 else out.at[pl.ds(pl.multiple_of(q * SUB + z * 128, 128), 128)]
        for distance in (2, 1, 3):
            copy = pltpu.make_async_remote_copy(
                src_ref=third.at[q], dst_ref=target, send_sem=s4.at[q, distance - 1], recv_sem=r4.at[q, distance - 1],
                device_id=along("z", distance), device_id_type=MESH)
            copy.start()
            last_copies[q, distance] = copy
        keep = pltpu.make_async_copy(third.at[q], target, own.at[q, 0])
        keep.start()
        last_copies[q, 0] = keep

    for q in (2, 0, 1, 3):
        for copy in local[q]:
            copy.wait()
        for j in range(len(hops)):
            for copy in first[q, j]:
                copy.wait()
        add_up(q)
        start_second(q)
    for q in (2, 0, 1, 3):
        start_third(q)
    for q in (2, 0, 1, 3):
        start_last(q)
    for distance in range(4):
        last_copies[2, distance].wait()
    spread = []
    target = out.at[pl.ds(pl.multiple_of(2 * SUB + x * 128, 128), 128)]
    for distance in (2, 1, 3):
        copy = pltpu.make_async_remote_copy(
            src_ref=crossed.at[(x + distance) % 4], dst_ref=target, send_sem=s5.at[distance - 1],
            recv_sem=r5.at[distance - 1], device_id=along("x", distance), device_id_type=MESH)
        copy.start()
        spread.append(copy)
    keep = pltpu.make_async_copy(crossed.at[x], target, own.at[2, 1])
    keep.start()
    spread.append(keep)
    for q in (0, 1, 3):
        for distance in range(4):
            last_copies[q, distance].wait()
    for copy in spread:
        copy.wait()


def reduce_call(rows, labels):
    dma = pltpu.SemaphoreType.DMA
    return pl.pallas_call(
        reduce_kernel,
        out_shape=jax.ShapeDtypeStruct((4 * SUB, WIDTH), F32),
        in_specs=[pl.BlockSpec(memory_space=pl.ANY)] * 2,
        out_specs=pl.BlockSpec(memory_space=pl.ANY),
        scratch_shapes=[
            pltpu.VMEM((4, 8, 4, 2 * CAP, 128), BF16),
            pltpu.VMEM((4, 8, 4, CAP), I32),
            pltpu.VMEM((4, 4, SUB, WIDTH), F32),
            pltpu.VMEM((4, 3, SUB, WIDTH), F32),
            pltpu.VMEM((4, SUB, WIDTH), F32),
            pltpu.VMEM((4, 3, 128, WIDTH), F32),
            pltpu.VMEM((4, 128, WIDTH), F32),
            pltpu.VMEM((4, 128, WIDTH), F32),
            dma((4, 7)), dma((4, 7)), dma((4, 7)), dma((4, 7)),
            dma((4, 3)), dma((4, 3)), dma((4, 3)), dma((4, 3)), dma((4, 3)), dma((4, 3)),
            dma((3,)), dma((3,)), dma((4, 2)),
        ],
        compiler_params=pltpu.CompilerParams(
            collective_id=0, has_side_effects=True, vmem_limit_bytes=56 << 20),
    )(rows, labels)


def local(embeddings, route, offset, centroids):
    slots, labels, counts, pairs = index_call(
        route.reshape(CHUNKS, CHUNK), offset.reshape(CHUNKS, CHUNK), embeddings)
    counts = lax.psum_scatter(counts.reshape(K), "cent", scatter_dimension=0, tiled=True)
    counts = lax.psum(counts, "sample")
    packed = place_call(slots.reshape(ROWS), pairs.reshape(ROWS, 2, 128))
    sums = reduce_call(packed.reshape(4, 8, 4, 2 * CAP, 128), labels.reshape(4, 8, 4, CAP))
    safe = jnp.maximum(counts, 1.0)
    return jnp.where(counts[:, None] > 0.0, sums / safe[:, None], centroids)


def solution(mesh):
    in_specs = (
        P(("sample", "cent"), None),
        P(("sample", "cent"), None),
        P(("sample", "cent")),
        P("cent", None),
    )
    return jax.shard_map(local, mesh=mesh, in_specs=in_specs, out_specs=P("cent", None), check_vma=False)
```

```python
import functools

import jax
import jax.numpy as jnp
from jax import lax
from jax.experimental import pallas as pl
from jax.experimental.pallas import tpu as pltpu
from jax.sharding import PartitionSpec as P

MESH = pl.DeviceIdType.MESH
K = 65536
WIDTH = 256
ROUTES = 128
SUB = 512
CAP = 256
ROWS = 16384
CHUNK = 1024
CHUNKS = ROWS // CHUNK
SLOTS = ROUTES * CAP
PART = 1024
F32, BF16, I32, I16 = jnp.float32, jnp.bfloat16, jnp.int32, jnp.int16
UNIT = 128


def place_of(route):
    quarter = route & 3
    core = (route >> 2) & 1
    y = (route >> 3) & 3
    x = route >> 5
    by_y = (quarter == 1) | ((quarter == 3) & (core == 1))
    ring = jnp.where(by_y, y, x)
    other = jnp.where(by_y, x, y)
    return quarter * 32 + ring * 8 + core * 4 + other


def pack_kernel(route, offset, x, packed_out, labels, rows, woven, packed, blank, slots, slots_s,
                upper, weave, base, found, in_sem, zero_sem, out_sem, slot_sem):
    def load(chunk):
        span = pl.ds(pl.multiple_of(chunk * CHUNK, CHUNK), CHUNK)
        return pltpu.make_async_copy(x.at[span], rows.at[span], in_sem.at[chunk])

    def clear(part):
        span = pl.ds(pl.multiple_of(part * PART, PART), PART)
        return pltpu.make_async_copy(blank, packed.at[span], zero_sem.at[part])

    def send(part):
        span = pl.ds(pl.multiple_of(part * PART, PART), PART)
        return pltpu.make_async_copy(packed.at[span], packed_out.at[span], out_sem.at[part])

    def slot_copy(turn):
        return pltpu.make_async_copy(slots.at[turn], slots_s.at[turn], slot_sem.at[turn])

    def each(count, act):
        def body(i, _):
            act(i)
            return 0
        lax.fori_loop(0, count, body, 0)

    blank[...] = jnp.zeros_like(blank)
    each(2, lambda i: load(i).start())
    each(SLOTS // PART, lambda i: clear(i).start())
    each(CHUNKS - 2, lambda i: load(i + 2).start())

    row = lax.broadcasted_iota(I32, (256, 256), 0)
    col = lax.broadcasted_iota(I32, (256, 256), 1)
    upper[...] = (row < col).astype(F32).astype(BF16)
    weave[...] = (col == (row >> 1) + (row & 1) * 128).astype(F32).astype(BF16)
    base[...] = jnp.zeros_like(base)
    found[...] = jnp.zeros_like(found)
    routes = lax.broadcasted_iota(I32, (ROUTES, CHUNK), 0)
    ranks = lax.broadcasted_iota(I32, (CHUNK, CAP), 1)

    def look(chunk, turn, between):
        at = pl.ds(chunk, 1)
        named = route[at, :]
        within = offset[at, :]
        place = place_of(named)
        mark = routes == place
        mark_f = mark.astype(F32)
        mark_b = mark_f.astype(BF16)
        between(0)
        start = base[:, :1]
        before = []
        for part in range(CHUNK // 256):
            cut = slice(part * 256, part * 256 + 256)
            before.append(jnp.dot(mark_b[:, cut], upper[...], preferred_element_type=F32) + start)
            start = start + jnp.sum(mark_f[:, cut], axis=1, keepdims=True)
        base[...] = jnp.broadcast_to(start, base.shape)
        rank = jnp.sum(jnp.where(mark, jnp.concatenate(before, axis=1), 0.0), axis=0, keepdims=True)
        slots[turn] = place * CAP + rank.astype(I32)
        between(1)
        for part in range(CHUNK // 256):
            first = pl.multiple_of(chunk * CHUNK + part * 256, 256)
            block = rows[pl.ds(first, 256), :]
            stacked = jnp.concatenate([
                jnp.concatenate([block[:128, :128], block[:128, 128:]], axis=0),
                jnp.concatenate([block[128:, :128], block[128:, 128:]], axis=0)], axis=1)
            mixed = jnp.dot(weave[...], stacked, preferred_element_type=F32).astype(BF16)
            woven[turn, part * 512:part * 512 + 256, :] = mixed[:, :128]
            woven[turn, part * 512 + 256:part * 512 + 512, :] = mixed[:, 128:]
            if part % 2:
                between(2 + part // 2)
        lines = jnp.concatenate([rank, within.astype(F32), jnp.zeros((6, CHUNK), F32)], axis=0)
        columns = lines.T
        within_f = columns[:, 1:2]
        value = jnp.where(ranks == columns[:, 0:1].astype(I32), within_f - 256.0, 0.0).astype(BF16)
        between(4)
        found[...] += jnp.dot(mark_b, value, preferred_element_type=F32)
        between(5)
        between(6)
        between(7)

    def move(turn, piece):
        for j in range(piece * (CHUNK // 8), (piece + 1) * (CHUNK // 8)):
            packed[slots_s[turn, 0, j]] = woven[turn, 2 * j:2 * j + 2, :]

    def ahead(chunk, _):
        load(chunk).wait()
        look(chunk, chunk, lambda piece: None)
        slot_copy(chunk).start()
        return 0

    def both(chunk, _):
        load(chunk).wait()
        turn = chunk % 3
        old = (chunk + 1) % 3
        slot_copy(old).wait()
        look(chunk, turn, lambda piece: move(old, piece))
        slot_copy(turn).start()
        return 0

    def behind(chunk, _):
        old = chunk % 3
        slot_copy(old).wait()

        for piece in range(8):
            move(old, piece)
        return 0

    lax.fori_loop(0, 2, ahead, 0)
    each(SLOTS // PART, lambda i: clear(i).wait())
    lax.fori_loop(2, CHUNKS, both, 0)
    lax.fori_loop(CHUNKS - 2, CHUNKS, behind, 0)
    each(SLOTS // PART, lambda i: send(i).start())
    lanes = lax.broadcasted_iota(I32, (ROUTES, CAP), 1)
    labels[...] = jnp.where(lanes < base[:, :1].astype(I32), found[...].astype(I32) + 256, -1)
    each(SLOTS // PART, lambda i: send(i).wait())


def pack_call(route, offset, x):
    vmem = pl.BlockSpec(memory_space=pltpu.VMEM)
    hbm = pl.BlockSpec(memory_space=pl.ANY)
    dma = pltpu.SemaphoreType.DMA
    return pl.pallas_call(
        pack_kernel,
        out_shape=[
            jax.ShapeDtypeStruct((SLOTS, 2, 128), BF16),
            jax.ShapeDtypeStruct((ROUTES, CAP), I32),
        ],
        in_specs=[vmem, vmem, hbm],
        out_specs=[hbm, vmem],
        scratch_shapes=[
            pltpu.VMEM((ROWS, WIDTH), BF16),
            pltpu.VMEM((3, 2 * CHUNK, 128), BF16),
            pltpu.VMEM((SLOTS, 2, 128), BF16),
            pltpu.VMEM((PART, 2, 128), BF16),
            pltpu.VMEM((3, 1, CHUNK), I32),
            pltpu.SMEM((3, 1, CHUNK), I32),
            pltpu.VMEM((256, 256), BF16),
            pltpu.VMEM((256, 256), BF16),
            pltpu.VMEM((ROUTES, 128), F32),
            pltpu.VMEM((ROUTES, CAP), F32),
            dma((CHUNKS,)), dma((SLOTS // PART,)), dma((SLOTS // PART,)), dma((3,)),
        ],
        compiler_params=pltpu.CompilerParams(vmem_limit_bytes=60 << 20),
    )(route, offset, x)


def device_at(x, y, z, core):
    return {"sample": z, "cent": (x * 4 + y) * 2 + core}


def encode(ref, value, count):
    eye = lax.broadcasted_iota(I32, (UNIT, UNIT), 0) == lax.broadcasted_iota(I32, (UNIT, UNIT), 1)
    top = jnp.max(jnp.abs(value), axis=1, keepdims=True)
    level = jnp.ceil(jnp.log2(jnp.maximum(top, 2.0 ** -90)) * 256.0) + 1.0
    ref[:UNIT, :] = jnp.round(value * (jnp.exp2(level * (-1.0 / 256.0)) * 32767.0)).astype(I32).astype(I16)
    line = jnp.sum(jnp.where(eye, level, 0.0), axis=0, keepdims=True)
    both = jnp.concatenate([line, count], axis=1)
    ref[UNIT:, :] = jnp.broadcast_to(both, (16, WIDTH)).astype(I32).astype(I16)


def upright(line):
    eye = lax.broadcasted_iota(I32, (UNIT, UNIT), 0) == lax.broadcasted_iota(I32, (UNIT, UNIT), 1)
    return jnp.sum(jnp.where(eye, line, 0.0), axis=1, keepdims=True)


def decode(ref):
    last = ref[UNIT:, :].astype(I32).astype(F32)
    level = upright(last[0:1, :UNIT])
    return ref[:UNIT, :].astype(I32).astype(F32) * (jnp.exp2(level * (1.0 / 256.0)) * (1.0 / 32767.0)), last[0:1, UNIT:]


def reduce_kernel(rows, labels, centroids, out, got, got_labels, total_s, count_s, kept, kept_count, sent2, got2,
                  sent3, got3, got4, got5, old, s1, r1, sl, rl, s2, r2, s3, r3, s4, r4, s5, r5, own, old_sem):
    z = lax.axis_index("sample")
    cent = lax.axis_index("cent")
    x, y, core = cent // 8, (cent // 2) % 4, cent % 2
    at = {"x": x, "y": y, "z": z}

    def along(axis, distance, core_to=None):
        to = dict(at)
        to[axis] = (to[axis] + distance) % 4
        return device_at(to["x"], to["y"], to["z"], core if core_to is None else core_to)

    def by_core(distance):
        return device_at((x + distance * core) % 4, (y + distance * (1 - core)) % 4, z, core)

    barrier = pltpu.get_barrier_semaphore()
    other = (core + 1) % 2
    pl.semaphore_signal(barrier, inc=1, device_id=device_at(x, y, z, other), device_id_type=MESH)
    for axis in "xyz":
        for distance in (1, 2, 3):
            for core_to in (core, other):
                pl.semaphore_signal(barrier, inc=1, device_id=along(axis, distance, core_to), device_id_type=MESH)
    pl.semaphore_wait(barrier, 19)

    hops = [(2, 0), (2, 1), (1, 0), (3, 0), (1, 1), (3, 1), (0, 1)]

    def first_copy(src, dst, ss, rs, q, j, step=None):
        distance, flip = hops[j]
        core_to = (core + flip) % 2
        if q == 3:
            ring = x * (1 - core_to) + y * core_to
            other_at = y * (1 - core_to) + x * core_to
            device = device_at((x + distance * (1 - core_to)) % 4, (y + distance * core_to) % 4, z, core_to)
        else:
            ring = at["xyz"[q]]
            other_at = at["yxy"[q]]
            device = along("xyz"[q], distance, core_to)
        to = ((ring + distance) % 4) * 2 + core_to
        mine = ring * 2 + core
        if step is None:
            src, dst, ss, rs = src.at[q, to], dst.at[q, mine], ss.at[q, j], rs.at[q, j]
        else:
            block = (other_at + step + 1) % 4
            src, dst, ss, rs = src.at[q, to, block], dst.at[q, mine, block], ss.at[q, j, step], rs.at[q, j, step]
        return pltpu.make_async_remote_copy(
            src_ref=src, dst_ref=dst, send_sem=ss, recv_sem=rs, device_id=device, device_id_type=MESH)

    def row_copy(q, j, step):
        return first_copy(rows, got, s1, r1, q, j, step)

    def label_copy(q, j):
        return first_copy(labels, got_labels, sl, rl, q, j)

    def start_rows(q, step):
        for j in range(len(hops)):
            row_copy(q, j, step).start()

    every = (0, 1, 2, 3)
    for q in every:
        for j in range(len(hops)):
            label_copy(q, j).start()

    def start_three(step, _):
        for q in (0, 1, 2):
            start_rows(q, step)
        return 0

    def start_fourth(step, _):
        start_rows(3, step)
        return 0

    lax.fori_loop(0, 4, start_three, 0)
    local = {}
    for q in every:
        ring = x * (1 - core) + y * core if q == 3 else at["xyz"[q]]
        mine = ring * 2 + core
        local[q] = [pltpu.make_async_copy(rows.at[q, mine], got.at[q, mine], own.at[q, 0]),
                    pltpu.make_async_copy(labels.at[q, mine], got_labels.at[q, mine], own.at[q, 1])]
        for copy in local[q]:
            copy.start()

    split_row = lax.broadcasted_iota(I32, (256, 256), 0)
    split_col = lax.broadcasted_iota(I32, (256, 256), 1)
    split = (split_col == (split_row % 128) * 2 + split_row // 128).astype(F32).astype(BF16)
    centroid = lax.broadcasted_iota(I32, (SUB, CAP), 0)
    eye = lax.broadcasted_iota(I32, (UNIT, UNIT), 0) == lax.broadcasted_iota(I32, (UNIT, UNIT), 1)
    second_axis = {0: "z", 1: "x", 2: "y"}
    second_at = {0: z, 1: x, 2: y, 3: y * (1 - core) + x * core}

    def second_copy(q, step, distance, block):
        if q == 0:
            src, dst = sent2.at[q, (z + distance) % 4, block], got2.at[q, distance - 1, block]
            number, device = distance - 1, along("z", distance)
        else:
            src, dst, number = sent2.at[q, step], got2.at[q, step], 0
            device = by_core(distance) if q == 3 else along(second_axis[q], distance)
        return pltpu.make_async_remote_copy(
            src_ref=src, dst_ref=dst, send_sem=s2.at[q, step, number], recv_sem=r2.at[q, step, number],
            device_id=device, device_id_type=MESH)

    def block_of(q, step):
        return ((y if q == 0 else second_at[q]) + step + 1) % 4

    def add_up(q, step):
        for j in range(len(hops)):
            row_copy(q, j, step).wait()
        block = block_of(q, step)
        flats, hits, tally = [], [], None
        for src in range(8):
            for half in range(2):
                both = jnp.dot(split, got[q, src, block, half * 256:(half + 1) * 256, :], preferred_element_type=F32).astype(BF16)
                flats.append(jnp.concatenate([both[:128], both[128:]], axis=1))
            name = got_labels[q, src, pl.ds(block, 1), :]
            hit = (centroid == name).astype(F32)
            tally = hit if tally is None else tally + hit
            hits.append(hit.astype(BF16))
        total_s[...] = jnp.dot(
            jnp.concatenate(hits, axis=1), jnp.concatenate(flats, axis=0), preferred_element_type=F32)
        column = jnp.sum(tally, axis=1, keepdims=True)
        for part in range(4):
            count = jnp.sum(jnp.where(eye, column[part * UNIT:(part + 1) * UNIT], 0.0), axis=0, keepdims=True)
            count_s[part] = jnp.broadcast_to(count, (8, UNIT))
        if q == 0:
            for part in range(4):
                encode(sent2.at[q, part, block], total_s[part * UNIT:(part + 1) * UNIT, :], count_s[part, 0:1, :])
            kept[q, block] = total_s[pl.ds(pl.multiple_of(z * UNIT, UNIT), UNIT), :]
            kept_count[q, block] = count_s[z]
            for distance in (2, 1, 3):
                second_copy(q, step, distance, block).start()
        else:
            @pl.when(step < 3)
            def _():
                for part in range(4):
                    encode(sent2.at[q, step, part], total_s[part * UNIT:(part + 1) * UNIT, :], count_s[part, 0:1, :])
                second_copy(q, step, step + 1, block).start()

            @pl.when(step == 3)
            def _():
                for part in range(4):
                    kept[q, part] = total_s[part * UNIT:(part + 1) * UNIT, :]
                    kept_count[q, part] = count_s[part]

    third_axis = {0: "y", 1: "z", 2: "x", 3: "z"}
    third_copies = {}

    def start_third(q):
        if q == 0:
            for step in range(4):
                for distance in (2, 1, 3):
                    second_copy(q, step, distance, block_of(q, step)).wait()
        else:
            for step in range(3):
                second_copy(q, step, step + 1, block_of(q, step)).wait()

        def join(part, _):
            value, count = kept[q, part], kept_count[q, part]
            for source in range(3):
                more, number = decode(got2.at[q, source, part])
                value, count = value + more, count + number
            kept[q, part] = value
            kept_count[q, part] = count
            encode(sent3.at[q, part], value, count[0:1, :])
            return 0

        lax.fori_loop(0, 4, join, 0)
        here = at[third_axis[q]]
        for distance in (2, 1, 3):
            copy = pltpu.make_async_remote_copy(
                src_ref=sent3.at[q, (here + distance) % 4], dst_ref=got3.at[q, distance - 1],
                send_sem=s3.at[q, distance - 1], recv_sem=r3.at[q, distance - 1],
                device_id=along(third_axis[q], distance), device_id_type=MESH)
            copy.start()
            third_copies[q, distance] = copy

    last_copies = {}

    def start_last(q):
        here = at[third_axis[q]]
        for distance in (2, 1, 3):
            third_copies[q, distance].wait()
        value, count = kept[q, here], kept_count[q, here]
        for source in range(3):
            more, number = decode(got3.at[q, source])
            value, count = value + more, count + number
        count = count[0:1, :]
        encode(got4.at[q, z], value / jnp.maximum(upright(count), 1.0), jnp.minimum(count, 1.0))
        for distance in (2, 1, 3):
            copy = pltpu.make_async_remote_copy(
                src_ref=got4.at[q, z], dst_ref=got4.at[q, z], send_sem=s4.at[q, distance - 1],
                recv_sem=r4.at[q, distance - 1], device_id=along("z", distance), device_id_type=MESH)
            copy.start()
            last_copies[q, distance] = copy

    spread = []

    def start_spread():
        for distance in (1, 2, 3):
            last_copies[2, distance].wait()
        for distance in (2, 1, 3):
            copy = pltpu.make_async_remote_copy(
                src_ref=got4.at[2, (x + distance) % 4], dst_ref=got5.at[x], send_sem=s5.at[distance - 1],
                recv_sem=r5.at[distance - 1], device_id=along("x", distance), device_id_type=MESH)
            copy.start()
            spread.append(copy)
        got5[x] = got4[2, x]

    def finish(q):
        if q == 2:
            for copy in spread:
                copy.wait()
        else:
            for distance in (1, 2, 3):
                last_copies[q, distance].wait()

        def part_out(part, _):
            value, count = decode(got5.at[part] if q == 2 else got4.at[q, part])
            span = pl.ds(pl.multiple_of(q * SUB + part * UNIT, UNIT), UNIT)
            out[span, :] = jnp.where(upright(count) > 0.0, value, old[span, :])
            return 0

        lax.fori_loop(0, 4, part_out, 0)

    old_copy = pltpu.make_async_copy(centroids, old, old_sem)
    old_copy.start()
    for q in every:
        for copy in local[q]:
            copy.wait()
        for j in range(len(hops)):
            label_copy(q, j).wait()

    def add_three(step, _):
        for q in (0, 1, 2):
            add_up(q, step)

        @pl.when(step == 2)
        def _():
            lax.fori_loop(0, 4, start_fourth, 0)

        return 0

    def add_fourth(step, _):
        add_up(3, step)
        return 0

    lax.fori_loop(0, 4, add_three, 0)
    lax.fori_loop(0, 1, add_fourth, 0)
    for q in (2, 0, 1):
        start_third(q)
    lax.fori_loop(1, 3, add_fourth, 0)
    for q in (2, 0, 1):
        start_last(q)
    lax.fori_loop(3, 4, add_fourth, 0)
    start_spread()
    old_copy.wait()
    start_third(3)
    finish(0)
    finish(1)
    start_last(3)
    finish(2)
    finish(3)


def reduce_call(rows, labels, centroids):
    dma = pltpu.SemaphoreType.DMA
    any_space = pl.BlockSpec(memory_space=pl.ANY)
    return pl.pallas_call(
        reduce_kernel,
        out_shape=jax.ShapeDtypeStruct((4 * SUB, WIDTH), F32),
        in_specs=[any_space] * 3,
        out_specs=pl.BlockSpec(memory_space=pltpu.VMEM),
        scratch_shapes=[
            pltpu.VMEM((4, 8, 4, 2 * CAP, 128), BF16),
            pltpu.VMEM((4, 8, 4, CAP), I32),
            pltpu.VMEM((SUB, WIDTH), F32),
            pltpu.VMEM((4, 8, UNIT), F32),
            pltpu.VMEM((4, 4, UNIT, WIDTH), F32),
            pltpu.VMEM((4, 4, 8, UNIT), F32),
            pltpu.VMEM((4, 4, 4, UNIT + 16, WIDTH), I16),
            pltpu.VMEM((4, 3, 4, UNIT + 16, WIDTH), I16),
            pltpu.VMEM((4, 4, UNIT + 16, WIDTH), I16),
            pltpu.VMEM((4, 3, UNIT + 16, WIDTH), I16),
            pltpu.VMEM((4, 4, UNIT + 16, WIDTH), I16),
            pltpu.VMEM((4, UNIT + 16, WIDTH), I16),
            pltpu.VMEM((4 * SUB, WIDTH), F32),
            dma((4, 7, 4)), dma((4, 7, 4)), dma((4, 7)), dma((4, 7)),
            dma((4, 4, 3)), dma((4, 4, 3)), dma((4, 3)), dma((4, 3)), dma((4, 3)), dma((4, 3)),
            dma((3,)), dma((3,)), dma((4, 2)), dma,
        ],
        compiler_params=pltpu.CompilerParams(
            collective_id=0, has_side_effects=True, vmem_limit_bytes=60 << 20),
    )(rows, labels, centroids)


def local(embeddings, route, offset, centroids):
    packed, labels = pack_call(
        route.reshape(CHUNKS, CHUNK), offset.reshape(CHUNKS, CHUNK), embeddings)
    return reduce_call(packed.reshape(4, 8, 4, 2 * CAP, 128), labels.reshape(4, 8, 4, CAP), centroids)


def solution(mesh):
    in_specs = (
        P(("sample", "cent"), None),
        P(("sample", "cent"), None),
        P(("sample", "cent")),
        P("cent", None),
    )
    return jax.shard_map(local, mesh=mesh, in_specs=in_specs, out_specs=P("cent", None), check_vma=False)
```

```python
import functools

import jax
import jax.numpy as jnp
from jax import lax
from jax.experimental import pallas as pl
from jax.experimental.pallas import tpu as pltpu
from jax.sharding import PartitionSpec as P

MESH = pl.DeviceIdType.MESH
K = 65536
WIDTH = 256
ROUTES = 128
SUB = 512
CAP = 256
ROWS = 16384
CHUNK = 1024
CHUNKS = ROWS // CHUNK
SLOTS = ROUTES * CAP
PART = 1024
F32, BF16, I32, I16 = jnp.float32, jnp.bfloat16, jnp.int32, jnp.int16
UNIT = 128


def place_of(route):
    quarter = route & 3
    core = (route >> 2) & 1
    y = (route >> 3) & 3
    x = route >> 5
    by_y = (quarter == 1) | ((quarter == 3) & (core == 1))
    ring = jnp.where(by_y, y, x)
    other = jnp.where(by_y, x, y)
    return quarter * 32 + ring * 8 + core * 4 + other


def pack_kernel(route, offset, x, packed, labels, rows, woven, woven1, blank, slots, slots1, slots_s,
                slots_s1, upper, weave, base, found, in_sem, zero_sem, slot_sem):
    def load(chunk):
        span = pl.ds(pl.multiple_of(chunk * CHUNK, CHUNK), CHUNK)
        return pltpu.make_async_copy(x.at[span], rows.at[span], in_sem.at[chunk])

    def clear(part):
        span = pl.ds(pl.multiple_of(part * PART, PART), PART)
        return pltpu.make_async_copy(blank, packed.at[span], zero_sem.at[part])

    pairs, places, places_s = (woven, woven1), (slots, slots1), (slots_s, slots_s1)

    def slot_copy(turn):
        return pltpu.make_async_copy(places[turn], places_s[turn], slot_sem.at[turn])

    def each(count, act):
        def body(i, _):
            act(i)
            return 0
        lax.fori_loop(0, count, body, 0)

    blank[...] = jnp.zeros_like(blank)
    each(2, lambda i: load(i).start())
    each(SLOTS // PART, lambda i: clear(i).start())
    each(CHUNKS - 2, lambda i: load(i + 2).start())

    row = lax.broadcasted_iota(I32, (256, 256), 0)
    col = lax.broadcasted_iota(I32, (256, 256), 1)
    upper[...] = (row < col).astype(F32).astype(BF16)
    weave[...] = (col == (row >> 1) + (row & 1) * 128).astype(F32).astype(BF16)
    base[...] = jnp.zeros_like(base)
    found[...] = jnp.zeros_like(found)
    routes = lax.broadcasted_iota(I32, (ROUTES, CHUNK), 0)
    ranks = lax.broadcasted_iota(I32, (CHUNK, CAP), 1)

    def interleave(chunk, turn, part):
        first = pl.multiple_of(chunk * CHUNK + part * 256, 256)
        block = rows[pl.ds(first, 256), :]
        stacked = jnp.concatenate([
            jnp.concatenate([block[:128, :128], block[:128, 128:]], axis=0),
            jnp.concatenate([block[128:, :128], block[128:, 128:]], axis=0)], axis=1)
        mixed = jnp.dot(weave[...], stacked, preferred_element_type=F32).astype(BF16)
        pairs[turn][part * 512:part * 512 + 256, :] = mixed[:, :128]
        pairs[turn][part * 512 + 256:part * 512 + 512, :] = mixed[:, 128:]

    def look(chunk, turn, between):
        at = pl.ds(pl.multiple_of(chunk * CHUNK, CHUNK), CHUNK)
        named = route[:, at]
        within = offset[:, at]
        place = place_of(named)
        mark = routes == place
        mark_f = mark.astype(F32)
        mark_b = mark_f.astype(BF16)
        between(0)
        start = base[:, :1]
        before = []
        for part in range(CHUNK // 256):
            cut = slice(part * 256, part * 256 + 256)
            before.append(jnp.dot(mark_b[:, cut], upper[...], preferred_element_type=F32) + start)
            start = start + jnp.sum(mark_f[:, cut], axis=1, keepdims=True)
        base[...] = jnp.broadcast_to(start, base.shape)
        rank = jnp.sum(jnp.where(mark, jnp.concatenate(before, axis=1), 0.0), axis=0, keepdims=True)
        places[turn][...] = place * CAP + rank.astype(I32)
        between(1)
        lines = jnp.concatenate([rank, within.astype(F32), jnp.zeros((6, CHUNK), F32)], axis=0)
        columns = lines.T
        between(2)
        within_f = columns[:, 1:2]
        value = jnp.where(ranks == columns[:, 0:1].astype(I32), within_f - 256.0, 0.0).astype(BF16)
        between(3)
        found[...] += jnp.dot(mark_b, value, preferred_element_type=F32)

    def move(turn, piece):
        for j in range(piece * (CHUNK // 8), (piece + 1) * (CHUNK // 8)):
            packed[places_s[turn][0, j]] = pairs[turn][2 * j:2 * j + 2, :]

    def full(chunk, turn):
        load(chunk).wait()
        slot_copy(turn).wait()

        def between(piece):
            move(turn, piece * 2)
            interleave(chunk - 1, 1 - turn, piece)
            move(turn, piece * 2 + 1)

        look(chunk, turn, between)
        slot_copy(turn).start()

    def two(i, _):
        full(2 * i, 0)
        full(2 * i + 1, 1)
        return 0

    load(0).wait()
    look(0, 0, lambda piece: None)
    slot_copy(0).start()
    load(1).wait()
    look(1, 1, lambda piece: interleave(0, 0, piece))
    slot_copy(1).start()
    each(SLOTS // PART, lambda i: clear(i).wait())
    lax.fori_loop(1, CHUNKS // 2, two, 0)
    slot_copy(0).wait()
    for piece in range(8):
        if piece < 4:
            interleave(CHUNKS - 1, 1, piece)
        move(0, piece)
    slot_copy(1).wait()
    for piece in range(8):
        move(1, piece)
    lanes = lax.broadcasted_iota(I32, (ROUTES, CAP), 1)
    named = jnp.where(lanes < base[:, :1].astype(I32), found[...].astype(I32) + 256, -1)
    for four in range(ROUTES // 4):
        labels[four] = named[four * 4:four * 4 + 4, :]


def pack_call(route, offset, x):
    vmem = pl.BlockSpec(memory_space=pltpu.VMEM)
    hbm = pl.BlockSpec(memory_space=pl.ANY)
    dma = pltpu.SemaphoreType.DMA
    return pl.pallas_call(
        pack_kernel,
        out_shape=[
            pltpu.VMEM((SLOTS, 2, 128), BF16),
            jax.ShapeDtypeStruct((ROUTES // 4, 4, CAP), I32),
        ],
        in_specs=[vmem, vmem, hbm],
        out_specs=[vmem, vmem],
        scratch_shapes=[
            pltpu.VMEM((ROWS, WIDTH), BF16),
            pltpu.VMEM((2 * CHUNK, 128), BF16),
            pltpu.VMEM((2 * CHUNK, 128), BF16),
            pltpu.VMEM((PART, 2, 128), BF16),
            pltpu.VMEM((1, CHUNK), I32),
            pltpu.VMEM((1, CHUNK), I32),
            pltpu.SMEM((1, CHUNK), I32),
            pltpu.SMEM((1, CHUNK), I32),
            pltpu.VMEM((256, 256), BF16),
            pltpu.VMEM((256, 256), BF16),
            pltpu.VMEM((ROUTES, 128), F32),
            pltpu.VMEM((ROUTES, CAP), F32),
            dma((CHUNKS,)), dma((SLOTS // PART,)), dma((2,)),
        ],
        compiler_params=pltpu.CompilerParams(vmem_limit_bytes=40 << 20),
    )(route, offset, x)


def device_at(x, y, z, core):
    return {"sample": z, "cent": (x * 4 + y) * 2 + core}


def encode(ref, value, count):
    eye = lax.broadcasted_iota(I32, (UNIT, UNIT), 0) == lax.broadcasted_iota(I32, (UNIT, UNIT), 1)
    top = jnp.max(jnp.abs(value), axis=1, keepdims=True)
    level = jnp.ceil(jnp.log2(jnp.maximum(top, 2.0 ** -90)) * 256.0) + 1.0
    ref[:UNIT, :] = jnp.round(value * (jnp.exp2(level * (-1.0 / 256.0)) * 32767.0)).astype(I32).astype(I16)
    line = jnp.sum(jnp.where(eye, level, 0.0), axis=0, keepdims=True)
    both = jnp.concatenate([line, count], axis=1)
    ref[UNIT:, :] = jnp.broadcast_to(both, (16, WIDTH)).astype(I32).astype(I16)


def upright(line):
    eye = lax.broadcasted_iota(I32, (UNIT, UNIT), 0) == lax.broadcasted_iota(I32, (UNIT, UNIT), 1)
    return jnp.sum(jnp.where(eye, line, 0.0), axis=1, keepdims=True)


def decode(ref):
    last = ref[UNIT:, :].astype(I32).astype(F32)
    level = upright(last[0:1, :UNIT])
    return ref[:UNIT, :].astype(I32).astype(F32) * (jnp.exp2(level * (1.0 / 256.0)) * (1.0 / 32767.0)), last[0:1, UNIT:]


def reduce_kernel(rows, labels, centroids, out, got, got_labels, hits, flats, total_s, count_s, kept, kept_count, sent2, got2,
                  sent3, got3, got4, got5, old, s1, r1, sl, rl, s2, r2, s3, r3, s4, r4, s5, r5, own, old_sem):
    z = lax.axis_index("sample")
    cent = lax.axis_index("cent")
    x, y, core = cent // 8, (cent // 2) % 4, cent % 2
    at = {"x": x, "y": y, "z": z}

    def along(axis, distance, core_to=None):
        to = dict(at)
        to[axis] = (to[axis] + distance) % 4
        return device_at(to["x"], to["y"], to["z"], core if core_to is None else core_to)

    def by_core(distance):
        return device_at((x + distance * core) % 4, (y + distance * (1 - core)) % 4, z, core)

    barrier = pltpu.get_barrier_semaphore()
    other = (core + 1) % 2
    pl.semaphore_signal(barrier, inc=1, device_id=device_at(x, y, z, other), device_id_type=MESH)
    for axis in "xyz":
        for distance in (1, 2, 3):
            for core_to in (core, other):
                pl.semaphore_signal(barrier, inc=1, device_id=along(axis, distance, core_to), device_id_type=MESH)
    pl.semaphore_wait(barrier, 19)

    hops = [(2, 0), (2, 1), (1, 0), (3, 0), (1, 1), (3, 1), (0, 1)]

    def first_copy(src, dst, ss, rs, q, j, step=None):
        distance, flip = hops[j]
        core_to = (core + flip) % 2
        if q == 3:
            ring = x * (1 - core_to) + y * core_to
            other_at = y * (1 - core_to) + x * core_to
            device = device_at((x + distance * (1 - core_to)) % 4, (y + distance * core_to) % 4, z, core_to)
        else:
            ring = at["xyz"[q]]
            other_at = at["yxy"[q]]
            device = along("xyz"[q], distance, core_to)
        to = ((ring + distance) % 4) * 2 + core_to
        mine = ring * 2 + core
        if step is None:
            src, dst, ss, rs = src.at[q, to], dst.at[q, mine], ss.at[q, j], rs.at[q, j]
        else:
            block = (other_at + step + 1) % 4
            src, dst, ss, rs = src.at[q, to, block], dst.at[q, mine, block], ss.at[q, j, step], rs.at[q, j, step]
        return pltpu.make_async_remote_copy(
            src_ref=src, dst_ref=dst, send_sem=ss, recv_sem=rs, device_id=device, device_id_type=MESH)

    def row_copy(q, j, step):
        return first_copy(rows, got, s1, r1, q, j, step)

    def label_copy(q, j):
        return first_copy(labels, got_labels, sl, rl, q, j)

    def start_rows(q, step):
        for j in range(len(hops)):
            row_copy(q, j, step).start()

    every = (0, 1, 2, 3)
    for q in every:
        for j in range(len(hops)):
            label_copy(q, j).start()

    def start_three(step, _):
        for q in (0, 1, 2):
            start_rows(q, step)
        return 0

    def start_fourth(step, _):
        start_rows(3, step)
        return 0

    lax.fori_loop(0, 4, start_three, 0)
    local = {}
    for q in every:
        ring = x * (1 - core) + y * core if q == 3 else at["xyz"[q]]
        mine = ring * 2 + core
        local[q] = [pltpu.make_async_copy(rows.at[q, mine], got.at[q, mine], own.at[q, 0]),
                    pltpu.make_async_copy(labels.at[q, mine], got_labels.at[q, mine], own.at[q, 1])]
        for copy in local[q]:
            copy.start()

    split_row = lax.broadcasted_iota(I32, (256, 256), 0)
    split_col = lax.broadcasted_iota(I32, (256, 256), 1)
    split = (split_col == (split_row % 128) * 2 + split_row // 128).astype(F32).astype(BF16)
    centroid = lax.broadcasted_iota(I32, (SUB, CAP), 0)
    eye = lax.broadcasted_iota(I32, (UNIT, UNIT), 0) == lax.broadcasted_iota(I32, (UNIT, UNIT), 1)
    second_at = {2: y, 3: y * (1 - core) + x * core}

    def second_copy(q, step, distance, block):
        if q < 2:
            src, dst = sent2.at[q, (z + distance) % 4, block], got2.at[q, distance - 1, block]
            number, device = distance - 1, along("z", distance)
        else:
            src, dst, number = sent2.at[q, step], got2.at[q, step], 0
            device = by_core(distance) if q == 3 else along("y", distance)
        return pltpu.make_async_remote_copy(
            src_ref=src, dst_ref=dst, send_sem=s2.at[q, step, number], recv_sem=r2.at[q, step, number],
            device_id=device, device_id_type=MESH)

    def block_of(q, step):
        return ((at["yx"[q]] if q < 2 else second_at[q]) + step + 1) % 4

    def add_up(q, step):
        for j in range(len(hops)):
            row_copy(q, j, step).wait()
        block = block_of(q, step)
        tally = None
        for src in range(8):
            for half in range(2):
                both = jnp.dot(split, got[q, src, block, half * 256:(half + 1) * 256, :], preferred_element_type=F32).astype(BF16)
                first = src * CAP + half * 128
                flats[first:first + 128, :] = jnp.concatenate([both[:128], both[128:]], axis=1)
            name = got_labels[q, src, pl.ds(block, 1), :]
            hit = (centroid == name).astype(F32)
            tally = hit if tally is None else tally + hit
            hits[:, src * CAP:(src + 1) * CAP] = hit.astype(BF16)
        total_s[...] = jnp.dot(hits[...], flats[...], preferred_element_type=F32)
        column = jnp.sum(tally, axis=1, keepdims=True)
        for part in range(4):
            count = jnp.sum(jnp.where(eye, column[part * UNIT:(part + 1) * UNIT], 0.0), axis=0, keepdims=True)
            count_s[part] = jnp.broadcast_to(count, (8, UNIT))
        if q < 2:
            for part in range(4):
                encode(sent2.at[q, part, block], total_s[part * UNIT:(part + 1) * UNIT, :], count_s[part, 0:1, :])
            kept[q, block] = total_s[pl.ds(pl.multiple_of(z * UNIT, UNIT), UNIT), :]
            kept_count[q, block] = count_s[z]
            for distance in (2, 1, 3):
                second_copy(q, step, distance, block).start()
        else:
            @pl.when(step < 3)
            def _():
                for part in range(4):
                    encode(sent2.at[q, step, part], total_s[part * UNIT:(part + 1) * UNIT, :], count_s[part, 0:1, :])
                second_copy(q, step, step + 1, block).start()

            @pl.when(step == 3)
            def _():
                for part in range(4):
                    kept[q, part] = total_s[part * UNIT:(part + 1) * UNIT, :]
                    kept_count[q, part] = count_s[part]

    third_axis = {0: "y", 1: "x", 2: "x", 3: "z"}
    third_copies = {}

    def start_third(q):
        if q < 2:
            for step in range(4):
                for distance in (2, 1, 3):
                    second_copy(q, step, distance, block_of(q, step)).wait()
        else:
            for step in range(3):
                second_copy(q, step, step + 1, block_of(q, step)).wait()

        def join(part, _):
            value, count = kept[q, part], kept_count[q, part]
            for source in range(3):
                more, number = decode(got2.at[q, source, part])
                value, count = value + more, count + number
            kept[q, part] = value
            kept_count[q, part] = count
            encode(sent3.at[q, part], value, count[0:1, :])
            return 0

        lax.fori_loop(0, 4, join, 0)
        here = at[third_axis[q]]
        for distance in (2, 1, 3):
            copy = pltpu.make_async_remote_copy(
                src_ref=sent3.at[q, (here + distance) % 4], dst_ref=got3.at[q, distance - 1],
                send_sem=s3.at[q, distance - 1], recv_sem=r3.at[q, distance - 1],
                device_id=along(third_axis[q], distance), device_id_type=MESH)
            copy.start()
            third_copies[q, distance] = copy

    last_copies = {}

    def start_last(q):
        here = at[third_axis[q]]
        for distance in (2, 1, 3):
            third_copies[q, distance].wait()
        value, count = kept[q, here], kept_count[q, here]
        for source in range(3):
            more, number = decode(got3.at[q, source])
            value, count = value + more, count + number
        count = count[0:1, :]
        encode(got4.at[q, z], value / jnp.maximum(upright(count), 1.0), jnp.minimum(count, 1.0))
        for distance in (2, 1, 3):
            copy = pltpu.make_async_remote_copy(
                src_ref=got4.at[q, z], dst_ref=got4.at[q, z], send_sem=s4.at[q, distance - 1],
                recv_sem=r4.at[q, distance - 1], device_id=along("z", distance), device_id_type=MESH)
            copy.start()
            last_copies[q, distance] = copy

    spread = []

    def start_spread():
        for distance in (1, 2, 3):
            last_copies[2, distance].wait()
        for distance in (2, 1, 3):
            copy = pltpu.make_async_remote_copy(
                src_ref=got4.at[2, (x + distance) % 4], dst_ref=got5.at[x], send_sem=s5.at[distance - 1],
                recv_sem=r5.at[distance - 1], device_id=along("x", distance), device_id_type=MESH)
            copy.start()
            spread.append(copy)
        got5[x] = got4[2, x]

    def finish(q):
        if q == 2:
            for copy in spread:
                copy.wait()
        else:
            for distance in (1, 2, 3):
                last_copies[q, distance].wait()

        def part_out(part, _):
            value, count = decode(got5.at[part] if q == 2 else got4.at[q, part])
            span = pl.ds(pl.multiple_of(q * SUB + part * UNIT, UNIT), UNIT)
            out[span, :] = jnp.where(upright(count) > 0.0, value, old[span, :])
            return 0

        lax.fori_loop(0, 4, part_out, 0)

    old_copy = pltpu.make_async_copy(centroids, old, old_sem)
    old_copy.start()
    for q in every:
        for copy in local[q]:
            copy.wait()
        for j in range(len(hops)):
            label_copy(q, j).wait()

    def add_three(step, _):
        for q in (0, 1, 2):
            add_up(q, step)

        @pl.when(step == 2)
        def _():
            lax.fori_loop(0, 4, start_fourth, 0)

        return 0

    def add_fourth(step, _):
        add_up(3, step)
        return 0

    lax.fori_loop(0, 4, add_three, 0)
    lax.fori_loop(0, 1, add_fourth, 0)
    for q in (2, 0, 1):
        start_third(q)
    lax.fori_loop(1, 3, add_fourth, 0)
    for q in (2, 0, 1):
        start_last(q)
    lax.fori_loop(3, 4, add_fourth, 0)
    start_spread()
    old_copy.wait()
    start_third(3)
    finish(0)
    finish(1)
    start_last(3)
    finish(2)
    finish(3)


def reduce_call(rows, labels, centroids):
    dma = pltpu.SemaphoreType.DMA
    any_space = pl.BlockSpec(memory_space=pl.ANY)
    return pl.pallas_call(
        reduce_kernel,
        out_shape=pltpu.VMEM((4 * SUB, WIDTH), F32),
        in_specs=[pl.BlockSpec(memory_space=pltpu.VMEM), any_space, any_space],
        out_specs=pl.BlockSpec(memory_space=pltpu.VMEM),
        scratch_shapes=[
            pltpu.VMEM((4, 8, 4, 2 * CAP, 128), BF16),
            pltpu.VMEM((4, 8, 4, CAP), I32),
            pltpu.VMEM((SUB, 8 * CAP), BF16),
            pltpu.VMEM((8 * CAP, WIDTH), BF16),
            pltpu.VMEM((SUB, WIDTH), F32),
            pltpu.VMEM((4, 8, UNIT), F32),
            pltpu.VMEM((4, 4, UNIT, WIDTH), F32),
            pltpu.VMEM((4, 4, 8, UNIT), F32),
            pltpu.VMEM((4, 4, 4, UNIT + 16, WIDTH), I16),
            pltpu.VMEM((4, 3, 4, UNIT + 16, WIDTH), I16),
            pltpu.VMEM((4, 4, UNIT + 16, WIDTH), I16),
            pltpu.VMEM((4, 3, UNIT + 16, WIDTH), I16),
            pltpu.VMEM((4, 4, UNIT + 16, WIDTH), I16),
            pltpu.VMEM((4, UNIT + 16, WIDTH), I16),
            pltpu.VMEM((4 * SUB, WIDTH), F32),
            dma((4, 7, 4)), dma((4, 7, 4)), dma((4, 7)), dma((4, 7)),
            dma((4, 4, 3)), dma((4, 4, 3)), dma((4, 3)), dma((4, 3)), dma((4, 3)), dma((4, 3)),
            dma((3,)), dma((3,)), dma((4, 2)), dma,
        ],
        compiler_params=pltpu.CompilerParams(
            collective_id=0, has_side_effects=True, vmem_limit_bytes=44 << 20),
    )(rows, labels, centroids)


def local(embeddings, route, offset, centroids):
    packed, labels = pack_call(
        route.T, offset.reshape(1, ROWS), embeddings)
    packed = pltpu.with_memory_space_constraint(packed.reshape(4, 8, 4, 2 * CAP, 128), pltpu.VMEM)
    return reduce_call(packed, labels.reshape(4, 8, 4, CAP), centroids)


def solution(mesh):
    in_specs = (
        P(("sample", "cent"), None),
        P(("sample", "cent"), None),
        P(("sample", "cent")),
        P("cent", None),
    )
    return jax.shard_map(local, mesh=mesh, in_specs=in_specs, out_specs=P("cent", None), check_vma=False)
```

```python
import functools

import jax
import jax.numpy as jnp
from jax import lax
from jax.experimental import pallas as pl
from jax.experimental.pallas import tpu as pltpu
from jax.sharding import PartitionSpec as P

MESH = pl.DeviceIdType.MESH
K = 65536
WIDTH = 256
ROUTES = 128
SUB = 512
CAP = 256
ROWS = 16384
CHUNK = 2048
CHUNKS = ROWS // CHUNK
SLOTS = ROUTES * CAP
PART = 1024
F32, BF16, I32, I16 = jnp.float32, jnp.bfloat16, jnp.int32, jnp.int16
UNIT = 128


def place_of(route):
    quarter = route & 3
    core = (route >> 2) & 1
    y = (route >> 3) & 3
    x = route >> 5
    by_y = (quarter == 1) | ((quarter == 3) & (core == 1))
    ring = jnp.where(by_y, y, x)
    other = jnp.where(by_y, x, y)
    return quarter * 32 + ring * 8 + core * 4 + other


def pack_kernel(route, offset, x, packed, labels, rows, woven, woven1, blank, slots, slots1, slots_s,
                slots_s1, upper, weave, base, found, in_sem, zero_sem, slot_sem):
    def load(chunk):
        span = pl.ds(pl.multiple_of(chunk * CHUNK, CHUNK), CHUNK)
        return pltpu.make_async_copy(x.at[span], rows.at[span], in_sem.at[chunk])

    def clear(part):
        span = pl.ds(pl.multiple_of(part * PART, PART), PART)
        return pltpu.make_async_copy(blank, packed.at[span], zero_sem.at[part])

    pairs, places, places_s = (woven, woven1), (slots, slots1), (slots_s, slots_s1)

    def slot_copy(turn):
        return pltpu.make_async_copy(places[turn], places_s[turn], slot_sem.at[turn])

    def each(count, act):
        def body(i, _):
            act(i)
            return 0
        lax.fori_loop(0, count, body, 0)

    blank[...] = jnp.zeros_like(blank)
    each(2, lambda i: load(i).start())
    each(SLOTS // PART, lambda i: clear(i).start())
    each(CHUNKS - 2, lambda i: load(i + 2).start())

    row = lax.broadcasted_iota(I32, (256, 256), 0)
    col = lax.broadcasted_iota(I32, (256, 256), 1)
    upper[...] = (row < col).astype(F32).astype(BF16)
    weave[...] = (col == (row >> 1) + (row & 1) * 128).astype(F32).astype(BF16)
    base[...] = jnp.zeros_like(base)
    found[...] = jnp.zeros_like(found)
    routes = lax.broadcasted_iota(I32, (ROUTES, CHUNK), 0)
    ranks = lax.broadcasted_iota(I32, (CHUNK, CAP), 1)

    def interleave(chunk, turn, part):
        first = pl.multiple_of(chunk * CHUNK + part * 256, 256)
        block = rows[pl.ds(first, 256), :]
        stacked = jnp.concatenate([
            jnp.concatenate([block[:128, :128], block[:128, 128:]], axis=0),
            jnp.concatenate([block[128:, :128], block[128:, 128:]], axis=0)], axis=1)
        mixed = jnp.dot(weave[...], stacked, preferred_element_type=F32).astype(BF16)
        pairs[turn][part * 512:part * 512 + 256, :] = mixed[:, :128]
        pairs[turn][part * 512 + 256:part * 512 + 512, :] = mixed[:, 128:]

    def look(chunk, turn, between):
        at = pl.ds(pl.multiple_of(chunk * CHUNK, CHUNK), CHUNK)
        named = route[:, at]
        within = offset[:, at]
        place = place_of(named)
        mark = routes == place
        mark_f = mark.astype(F32)
        mark_b = mark_f.astype(BF16)
        between(0)
        start = base[:, :1]
        before = []
        for part in range(CHUNK // 256):
            cut = slice(part * 256, part * 256 + 256)
            before.append(jnp.dot(mark_b[:, cut], upper[...], preferred_element_type=F32) + start)
            start = start + jnp.sum(mark_f[:, cut], axis=1, keepdims=True)
        base[...] = jnp.broadcast_to(start, base.shape)
        rank = jnp.sum(jnp.where(mark, jnp.concatenate(before, axis=1), 0.0), axis=0, keepdims=True)
        places[turn][...] = place * CAP + rank.astype(I32)
        between(1)
        lines = jnp.concatenate([rank, within.astype(F32), jnp.zeros((6, CHUNK), F32)], axis=0)
        columns = lines.T
        between(2)
        within_f = columns[:, 1:2]
        value = jnp.where(ranks == columns[:, 0:1].astype(I32), within_f - 256.0, 0.0).astype(BF16)
        between(3)
        found[...] += jnp.dot(mark_b, value, preferred_element_type=F32)

    def move(turn, piece):
        for j in range(piece * (CHUNK // 8), (piece + 1) * (CHUNK // 8)):
            packed[places_s[turn][0, j]] = pairs[turn][2 * j:2 * j + 2, :]

    def full(chunk, turn):
        load(chunk).wait()
        slot_copy(turn).wait()

        def between(piece):
            move(turn, piece * 2)
            for part in range(piece * CHUNK // 1024, (piece + 1) * CHUNK // 1024):
                interleave(chunk - 1, 1 - turn, part)
            move(turn, piece * 2 + 1)

        look(chunk, turn, between)
        slot_copy(turn).start()

    def two(i, _):
        full(2 * i, 0)
        full(2 * i + 1, 1)
        return 0

    load(0).wait()
    look(0, 0, lambda piece: None)
    slot_copy(0).start()
    load(1).wait()
    look(1, 1, lambda piece: [interleave(0, 0, part) for part in range(piece * CHUNK // 1024, (piece + 1) * CHUNK // 1024)])
    slot_copy(1).start()
    each(SLOTS // PART, lambda i: clear(i).wait())
    lax.fori_loop(1, CHUNKS // 2, two, 0)
    slot_copy(0).wait()
    for piece in range(8):
        if piece < 4:
            for part in range(piece * CHUNK // 1024, (piece + 1) * CHUNK // 1024):
                interleave(CHUNKS - 1, 1, part)
        move(0, piece)
    slot_copy(1).wait()
    for piece in range(8):
        move(1, piece)
    lanes = lax.broadcasted_iota(I32, (ROUTES, CAP), 1)
    named = jnp.where(lanes < base[:, :1].astype(I32), found[...].astype(I32) + 256, -1)
    for four in range(ROUTES // 4):
        labels[four] = named[four * 4:four * 4 + 4, :]


def pack_call(route, offset, x):
    vmem = pl.BlockSpec(memory_space=pltpu.VMEM)
    hbm = pl.BlockSpec(memory_space=pl.ANY)
    dma = pltpu.SemaphoreType.DMA
    return pl.pallas_call(
        pack_kernel,
        out_shape=[
            pltpu.VMEM((SLOTS, 2, 128), BF16),
            jax.ShapeDtypeStruct((ROUTES // 4, 4, CAP), I32),
        ],
        in_specs=[vmem, vmem, hbm],
        out_specs=[vmem, vmem],
        scratch_shapes=[
            pltpu.VMEM((ROWS, WIDTH), BF16),
            pltpu.VMEM((2 * CHUNK, 128), BF16),
            pltpu.VMEM((2 * CHUNK, 128), BF16),
            pltpu.VMEM((PART, 2, 128), BF16),
            pltpu.VMEM((1, CHUNK), I32),
            pltpu.VMEM((1, CHUNK), I32),
            pltpu.SMEM((1, CHUNK), I32),
            pltpu.SMEM((1, CHUNK), I32),
            pltpu.VMEM((256, 256), BF16),
            pltpu.VMEM((256, 256), BF16),
            pltpu.VMEM((ROUTES, 128), F32),
            pltpu.VMEM((ROUTES, CAP), F32),
            dma((CHUNKS,)), dma((SLOTS // PART,)), dma((2,)),
        ],
        compiler_params=pltpu.CompilerParams(vmem_limit_bytes=40 << 20),
    )(route, offset, x)


def device_at(x, y, z, core):
    return {"sample": z, "cent": (x * 4 + y) * 2 + core}


def encode(ref, value, count):
    eye = lax.broadcasted_iota(I32, (UNIT, UNIT), 0) == lax.broadcasted_iota(I32, (UNIT, UNIT), 1)
    top = jnp.max(jnp.abs(value), axis=1, keepdims=True)
    level = jnp.ceil(jnp.log2(jnp.maximum(top, 2.0 ** -90)) * 256.0) + 1.0
    ref[:UNIT, :] = jnp.round(value * (jnp.exp2(level * (-1.0 / 256.0)) * 32767.0)).astype(I32).astype(I16)
    line = jnp.sum(jnp.where(eye, level, 0.0), axis=0, keepdims=True)
    both = jnp.concatenate([line, count], axis=1)
    ref[UNIT:, :] = jnp.broadcast_to(both, (16, WIDTH)).astype(I32).astype(I16)


def upright(line):
    eye = lax.broadcasted_iota(I32, (UNIT, UNIT), 0) == lax.broadcasted_iota(I32, (UNIT, UNIT), 1)
    return jnp.sum(jnp.where(eye, line, 0.0), axis=1, keepdims=True)


def decode(ref):
    last = ref[UNIT:, :].astype(I32).astype(F32)
    level = upright(last[0:1, :UNIT])
    return ref[:UNIT, :].astype(I32).astype(F32) * (jnp.exp2(level * (1.0 / 256.0)) * (1.0 / 32767.0)), last[0:1, UNIT:]


def reduce_kernel(rows, labels, centroids, out, got, got_labels, hits, flats, total_s, count_s, kept, kept_count, sent2, got2,
                  sent3, got3, got4, got5, old, s1, r1, sl, rl, s2, r2, s3, r3, s4, r4, s5, r5, own, old_sem):
    z = lax.axis_index("sample")
    cent = lax.axis_index("cent")
    x, y, core = cent // 8, (cent // 2) % 4, cent % 2
    at = {"x": x, "y": y, "z": z}

    def along(axis, distance, core_to=None):
        to = dict(at)
        to[axis] = (to[axis] + distance) % 4
        return device_at(to["x"], to["y"], to["z"], core if core_to is None else core_to)

    def by_core(distance):
        return device_at((x + distance * core) % 4, (y + distance * (1 - core)) % 4, z, core)

    barrier = pltpu.get_barrier_semaphore()
    other = (core + 1) % 2
    pl.semaphore_signal(barrier, inc=1, device_id=device_at(x, y, z, other), device_id_type=MESH)
    for axis in "xyz":
        for distance in (1, 2, 3):
            for core_to in (core, other):
                pl.semaphore_signal(barrier, inc=1, device_id=along(axis, distance, core_to), device_id_type=MESH)
    pl.semaphore_wait(barrier, 19)

    hops = [(2, 0), (2, 1), (1, 0), (3, 0), (1, 1), (3, 1), (0, 1)]

    def first_copy(src, dst, ss, rs, q, j, step=None):
        distance, flip = hops[j]
        core_to = (core + flip) % 2
        if q == 3:
            ring = x * (1 - core_to) + y * core_to
            other_at = y * (1 - core_to) + x * core_to
            device = device_at((x + distance * (1 - core_to)) % 4, (y + distance * core_to) % 4, z, core_to)
        else:
            ring = at["xyz"[q]]
            other_at = at["yxy"[q]]
            device = along("xyz"[q], distance, core_to)
        to = ((ring + distance) % 4) * 2 + core_to
        mine = ring * 2 + core
        if step is None:
            src, dst, ss, rs = src.at[q, to], dst.at[q, mine], ss.at[q, j], rs.at[q, j]
        else:
            block = (other_at + step + 1) % 4
            src, dst, ss, rs = src.at[q, to, block], dst.at[q, mine, block], ss.at[q, j, step], rs.at[q, j, step]
        return pltpu.make_async_remote_copy(
            src_ref=src, dst_ref=dst, send_sem=ss, recv_sem=rs, device_id=device, device_id_type=MESH)

    def row_copy(q, j, step):
        return first_copy(rows, got, s1, r1, q, j, step)

    def label_copy(q, j):
        return first_copy(labels, got_labels, sl, rl, q, j)

    def start_rows(q, step):
        for j in range(len(hops)):
            row_copy(q, j, step).start()

    every = (0, 1, 2, 3)
    for q in every:
        for j in range(len(hops)):
            label_copy(q, j).start()

    def start_three(step, _):
        for q in (0, 1, 2):
            start_rows(q, step)
        return 0

    def start_fourth(step, _):
        start_rows(3, step)
        return 0

    lax.fori_loop(0, 4, start_three, 0)
    local = {}
    for q in every:
        ring = x * (1 - core) + y * core if q == 3 else at["xyz"[q]]
        mine = ring * 2 + core
        local[q] = [pltpu.make_async_copy(rows.at[q, mine], got.at[q, mine], own.at[q, 0]),
                    pltpu.make_async_copy(labels.at[q, mine], got_labels.at[q, mine], own.at[q, 1])]
        for copy in local[q]:
            copy.start()

    split_row = lax.broadcasted_iota(I32, (256, 256), 0)
    split_col = lax.broadcasted_iota(I32, (256, 256), 1)
    split = (split_col == (split_row % 128) * 2 + split_row // 128).astype(F32).astype(BF16)
    centroid = lax.broadcasted_iota(I32, (SUB, CAP), 0)
    eye = lax.broadcasted_iota(I32, (UNIT, UNIT), 0) == lax.broadcasted_iota(I32, (UNIT, UNIT), 1)
    second_at = {2: y, 3: y * (1 - core) + x * core}

    def second_copy(q, step, distance, block):
        if q < 2:
            src, dst = sent2.at[q, (z + distance) % 4, block], got2.at[q, distance - 1, block]
            number, device = distance - 1, along("z", distance)
        else:
            src, dst, number = sent2.at[q, step], got2.at[q, step], 0
            device = by_core(distance) if q == 3 else along("y", distance)
        return pltpu.make_async_remote_copy(
            src_ref=src, dst_ref=dst, send_sem=s2.at[q, step, number], recv_sem=r2.at[q, step, number],
            device_id=device, device_id_type=MESH)

    def block_of(q, step):
        return ((at["yx"[q]] if q < 2 else second_at[q]) + step + 1) % 4

    def add_up(q, step):
        for j in range(len(hops)):
            row_copy(q, j, step).wait()
        block = block_of(q, step)
        tally = None
        for src in range(8):
            for half in range(2):
                both = jnp.dot(split, got[q, src, block, half * 256:(half + 1) * 256, :], preferred_element_type=F32).astype(BF16)
                first = src * CAP + half * 128
                flats[first:first + 128, :] = jnp.concatenate([both[:128], both[128:]], axis=1)
            name = got_labels[q, src, pl.ds(block, 1), :]
            hit = (centroid == name).astype(F32)
            tally = hit if tally is None else tally + hit
            hits[:, src * CAP:(src + 1) * CAP] = hit.astype(BF16)
        total_s[...] = jnp.dot(hits[...], flats[...], preferred_element_type=F32)
        column = jnp.sum(tally, axis=1, keepdims=True)
        for part in range(4):
            count = jnp.sum(jnp.where(eye, column[part * UNIT:(part + 1) * UNIT], 0.0), axis=0, keepdims=True)
            count_s[part] = jnp.broadcast_to(count, (8, UNIT))
        if q < 2:
            for part in range(4):
                encode(sent2.at[q, part, block], total_s[part * UNIT:(part + 1) * UNIT, :], count_s[part, 0:1, :])
            kept[q, block] = total_s[pl.ds(pl.multiple_of(z * UNIT, UNIT), UNIT), :]
            kept_count[q, block] = count_s[z]
            for distance in (2, 1, 3):
                second_copy(q, step, distance, block).start()
        else:
            @pl.when(step < 3)
            def _():
                for part in range(4):
                    encode(sent2.at[q, step, part], total_s[part * UNIT:(part + 1) * UNIT, :], count_s[part, 0:1, :])
                second_copy(q, step, step + 1, block).start()

            @pl.when(step == 3)
            def _():
                for part in range(4):
                    kept[q, part] = total_s[part * UNIT:(part + 1) * UNIT, :]
                    kept_count[q, part] = count_s[part]

    third_axis = {0: "y", 1: "x", 2: "x", 3: "z"}
    third_copies = {}

    def start_third(q):
        if q < 2:
            for step in range(4):
                for distance in (2, 1, 3):
                    second_copy(q, step, distance, block_of(q, step)).wait()
        else:
            for step in range(3):
                second_copy(q, step, step + 1, block_of(q, step)).wait()

        def join(part, _):
            value, count = kept[q, part], kept_count[q, part]
            for source in range(3):
                more, number = decode(got2.at[q, source, part])
                value, count = value + more, count + number
            kept[q, part] = value
            kept_count[q, part] = count
            encode(sent3.at[q, part], value, count[0:1, :])
            return 0

        lax.fori_loop(0, 4, join, 0)
        here = at[third_axis[q]]
        for distance in (2, 1, 3):
            copy = pltpu.make_async_remote_copy(
                src_ref=sent3.at[q, (here + distance) % 4], dst_ref=got3.at[q, distance - 1],
                send_sem=s3.at[q, distance - 1], recv_sem=r3.at[q, distance - 1],
                device_id=along(third_axis[q], distance), device_id_type=MESH)
            copy.start()
            third_copies[q, distance] = copy

    last_copies = {}

    def start_last(q):
        here = at[third_axis[q]]
        for distance in (2, 1, 3):
            third_copies[q, distance].wait()
        value, count = kept[q, here], kept_count[q, here]
        for source in range(3):
            more, number = decode(got3.at[q, source])
            value, count = value + more, count + number
        count = count[0:1, :]
        encode(got4.at[q, z], value / jnp.maximum(upright(count), 1.0), jnp.minimum(count, 1.0))
        for distance in (2, 1, 3):
            copy = pltpu.make_async_remote_copy(
                src_ref=got4.at[q, z], dst_ref=got4.at[q, z], send_sem=s4.at[q, distance - 1],
                recv_sem=r4.at[q, distance - 1], device_id=along("z", distance), device_id_type=MESH)
            copy.start()
            last_copies[q, distance] = copy

    spread = []

    def start_spread():
        for distance in (1, 2, 3):
            last_copies[2, distance].wait()
        for distance in (2, 1, 3):
            copy = pltpu.make_async_remote_copy(
                src_ref=got4.at[2, (x + distance) % 4], dst_ref=got5.at[x], send_sem=s5.at[distance - 1],
                recv_sem=r5.at[distance - 1], device_id=along("x", distance), device_id_type=MESH)
            copy.start()
            spread.append(copy)
        got5[x] = got4[2, x]

    def finish(q):
        if q == 2:
            for copy in spread:
                copy.wait()
        else:
            for distance in (1, 2, 3):
                last_copies[q, distance].wait()

        def part_out(part, _):
            value, count = decode(got5.at[part] if q == 2 else got4.at[q, part])
            span = pl.ds(pl.multiple_of(q * SUB + part * UNIT, UNIT), UNIT)
            out[span, :] = jnp.where(upright(count) > 0.0, value, old[span, :])
            return 0

        lax.fori_loop(0, 4, part_out, 0)

    old_copy = pltpu.make_async_copy(centroids, old, old_sem)
    old_copy.start()
    for q in every:
        for copy in local[q]:
            copy.wait()
        for j in range(len(hops)):
            label_copy(q, j).wait()

    def add_three(step, _):
        for q in (0, 1, 2):
            add_up(q, step)

        @pl.when(step == 2)
        def _():
            lax.fori_loop(0, 4, start_fourth, 0)

        return 0

    def add_fourth(step, _):
        add_up(3, step)
        return 0

    lax.fori_loop(0, 4, add_three, 0)
    lax.fori_loop(0, 1, add_fourth, 0)
    for q in (2, 0, 1):
        start_third(q)
    lax.fori_loop(1, 3, add_fourth, 0)
    for q in (2, 0, 1):
        start_last(q)
    lax.fori_loop(3, 4, add_fourth, 0)
    start_spread()
    old_copy.wait()
    start_third(3)
    finish(0)
    finish(1)
    start_last(3)
    finish(2)
    finish(3)


def reduce_call(rows, labels, centroids):
    dma = pltpu.SemaphoreType.DMA
    any_space = pl.BlockSpec(memory_space=pl.ANY)
    return pl.pallas_call(
        reduce_kernel,
        out_shape=pltpu.VMEM((4 * SUB, WIDTH), F32),
        in_specs=[pl.BlockSpec(memory_space=pltpu.VMEM), any_space, any_space],
        out_specs=pl.BlockSpec(memory_space=pltpu.VMEM),
        scratch_shapes=[
            pltpu.VMEM((4, 8, 4, 2 * CAP, 128), BF16),
            pltpu.VMEM((4, 8, 4, CAP), I32),
            pltpu.VMEM((SUB, 8 * CAP), BF16),
            pltpu.VMEM((8 * CAP, WIDTH), BF16),
            pltpu.VMEM((SUB, WIDTH), F32),
            pltpu.VMEM((4, 8, UNIT), F32),
            pltpu.VMEM((4, 4, UNIT, WIDTH), F32),
            pltpu.VMEM((4, 4, 8, UNIT), F32),
            pltpu.VMEM((4, 4, 4, UNIT + 16, WIDTH), I16),
            pltpu.VMEM((4, 3, 4, UNIT + 16, WIDTH), I16),
            pltpu.VMEM((4, 4, UNIT + 16, WIDTH), I16),
            pltpu.VMEM((4, 3, UNIT + 16, WIDTH), I16),
            pltpu.VMEM((4, 4, UNIT + 16, WIDTH), I16),
            pltpu.VMEM((4, UNIT + 16, WIDTH), I16),
            pltpu.VMEM((4 * SUB, WIDTH), F32),
            dma((4, 7, 4)), dma((4, 7, 4)), dma((4, 7)), dma((4, 7)),
            dma((4, 4, 3)), dma((4, 4, 3)), dma((4, 3)), dma((4, 3)), dma((4, 3)), dma((4, 3)),
            dma((3,)), dma((3,)), dma((4, 2)), dma,
        ],
        compiler_params=pltpu.CompilerParams(
            collective_id=0, has_side_effects=True, vmem_limit_bytes=44 << 20),
    )(rows, labels, centroids)


def local(embeddings, route, offset, centroids):
    packed, labels = pack_call(
        route.T, offset.reshape(1, ROWS), embeddings)
    packed = pltpu.with_memory_space_constraint(packed.reshape(4, 8, 4, 2 * CAP, 128), pltpu.VMEM)
    return reduce_call(packed, labels.reshape(4, 8, 4, CAP), centroids)


def solution(mesh):
    in_specs = (
        P(("sample", "cent"), None),
        P(("sample", "cent"), None),
        P(("sample", "cent")),
        P("cent", None),
    )
    return jax.shard_map(local, mesh=mesh, in_specs=in_specs, out_specs=P("cent", None), check_vma=False)
```
